512 devices in a mesh: section: 16 (over y_lo, z), tensor: 32 (over x, y_hi, core).
Axes of the slice: x: 4, y: 8 (y_hi: 4, y_lo: 2; y = y_hi * 2 + y_lo), z: 8, core: 2. Of those that a mesh axis runs over, the one named last changes fastest.
Arguments:
- x_down: bfloat16 [2, 16, 128, 4096], P(None, 'section', 'tensor'), may hold values from -6 to 6
- x_up: bfloat16 [2, 16, 128, 4096], P(None, 'section', 'tensor'), may hold values from -6 to 6
- g_down: bfloat16 [16, 128, 4096], P('section', 'tensor'), may hold values from -6 to 6
- g_up: bfloat16 [16, 128, 4096], P('section', 'tensor'), may hold values from -6 to 6
- loss_grad: bfloat16 [2, 128, 4096], P(None, 'tensor'), may hold values from -6 to 6
- w_in: bfloat16 [16, 4096, 4096], P('section', None, 'tensor'), may hold values from -1 to 1
- w_out: bfloat16 [16, 4096, 4096], P('section', 'tensor'), may hold values from -0.09375 to 0.09375
- gain: bfloat16 [16, 4096], P('section'), may hold values from 0.5 to 1.5
- retention: bfloat16 [16, 4096], P('section', 'tensor'), may hold values from 0.8984375 to 0.9921875
- layer_kind: int32 [16], replicated, may hold values from 0 to 1, as said below
Outputs:
- gx_down: bfloat16 [16, 128, 4096], P('section', 'tensor')
- gx_up: bfloat16 [16, 128, 4096], P('section', 'tensor')
- grad_in: bfloat16 [16, 4096, 4096], P('section', None, 'tensor')
- grad_out: bfloat16 [16, 4096, 4096], P('section', 'tensor')
The draws below stay inside these ranges and needn't reach their ends.
Inputs may be any that keep to these rules, and one draw needn't show every extreme that they name: `layer_kind`: each aligned group of 8 layers holds at least one attention layer and at least one recurrent layer.
All inputs are finite; a program needn't handle non-finite values.
Results may differ from the reference program's by a relative error of at most 0.039.
Values may be sent and summed in bfloat16 or wider, within the bound.
A program may use at most 128 MiB of HBM per device.

```python
import jax
import jax.numpy as jnp
from jax import lax

D = 4096
HEAD = 128
TOK = 128
TICKS = 2
LAYERS = 16
E = 4096


def layer_kinds(key):
    period = min(8, LAYERS)
    groups = (LAYERS + period - 1) // period
    base = jax.random.fold_in(key, 7)
    attention_at = jax.random.randint(jax.random.fold_in(base, 1), (groups,), 0, period)
    step_away = jax.random.randint(jax.random.fold_in(base, 2), (groups,), 1, period)
    recurrent_at = (attention_at + step_away) % period
    coins = jax.random.randint(jax.random.fold_in(base, 3), (LAYERS,), 0, 2)
    layer_index = jnp.arange(LAYERS)
    group_of = layer_index // period
    inside = layer_index % period
    forced_one = inside == attention_at[group_of]
    forced_zero = inside == recurrent_at[group_of]
    return jnp.where(forced_one, 1, jnp.where(forced_zero, 0, coins)).astype(jnp.int32)


def draw_layer_kind(key, part):
    return layer_kinds(key)


def drawn_tokens(key, seed_offset):
    return jax.random.truncated_normal(jax.random.fold_in(key, seed_offset), -6.0, 6.0, (TICKS, LAYERS, TOK, D), jnp.float32)


def draw_x_down(key, part):
    values = drawn_tokens(key, 11)
    return values.astype(jnp.bfloat16)


def draw_x_up(key, part):
    values = drawn_tokens(key, 12)
    return values.astype(jnp.bfloat16)


def draw_w_in(key, part):
    fan_scale = D ** (-0.5)
    values = jax.random.truncated_normal(jax.random.fold_in(key, 21), -6.0, 6.0, (LAYERS, D, E), jnp.float32)
    return (values * fan_scale).astype(jnp.bfloat16)


def block_levels(rng, extent, shards, least, largest):
    loudness = 1.0
    for position, blocks in shards:
        draws = jax.random.uniform(jax.random.fold_in(jax.random.fold_in(rng, 6), position), (blocks,), jnp.float32, least / len(shards), largest / len(shards))
        loudness = loudness * jnp.repeat(jnp.exp(draws), extent[position] // blocks).reshape((-1,) + (1,) * (len(extent) - 1 - position))
    return loudness


def normal_values(own_key, extent, scale, bound, shards=(), kind=jnp.bfloat16):
    array = scale * jax.random.normal(own_key, extent, jnp.float32)
    if shards:
        array = array * block_levels(own_key, extent, shards, -0.22, 0.18)
    return jnp.clip(array, -bound, bound).astype(kind)


def setup_inputs(seed: int = 0) -> dict:
    key_of = jax.random.split(jax.random.key(seed), 11)
    x_down = draw_x_down(jax.random.fold_in(key_of[10], 71), 0)
    x_up = draw_x_up(jax.random.fold_in(key_of[10], 71), 0)
    g_down = normal_values(key_of[2], (LAYERS, TOK, D), 1.0, 6.0, ((0, 16), (1, 32)))
    g_up = normal_values(key_of[3], (LAYERS, TOK, D), 1.0, 6.0, ((0, 16), (1, 32)))
    loss_grad = normal_values(key_of[4], (2, TOK, D), 1.0, 6.0, ((1, 32),))
    w_in = draw_w_in(jax.random.fold_in(key_of[10], 71), 0)
    w_out = normal_values(key_of[6], (LAYERS, E, D), E ** -0.5, 0.09375, ((0, 16), (1, 32)))
    gain = jnp.clip(1.0 + 0.1 * jax.random.normal(key_of[7], (LAYERS, D), jnp.float32), 0.5, 1.5).astype(jnp.bfloat16)
    retention = jnp.clip(0.8984375 + 0.09375 * jax.random.uniform(key_of[8], (LAYERS, E), jnp.float32) ** block_levels(key_of[8], (LAYERS, E), ((0, 16), (1, 32)), -0.2, 0.2), 0.8984375, 0.9921875).astype(jnp.bfloat16)
    layer_kind = draw_layer_kind(jax.random.fold_in(key_of[10], 71), 0)
    return dict(x_down=x_down, x_up=x_up, g_down=g_down, g_up=g_up, loss_grad=loss_grad, w_in=w_in, w_out=w_out, gain=gain, retention=retention, layer_kind=layer_kind)


EPSILON = 1e-05

def combine_steps(earlier, following):
    first_decay, first_state = earlier
    next_decay, next_state = following
    return (first_decay * next_decay, next_decay * first_state + next_state)

def mix_channels(projected, rates, kind):

    def recurrent(values_in):
        decay = jnp.broadcast_to(rates, values_in.shape)
        states = lax.associative_scan(combine_steps, (decay, (1.0 - rates) * values_in), axis=0)[1]
        return states * jax.nn.silu(values_in)

    def attend(values_in):
        half_width = values_in.shape[-1] // 2
        queries = values_in[..., :half_width]
        key_part = values_in[..., half_width:]
        scores = jnp.einsum('thd,shd->hts', queries, key_part, precision=lax.Precision.HIGHEST) * half_width ** (-0.5)
        length_now = values_in.shape[0]
        causal = jnp.arange(length_now)[:, None] >= jnp.arange(length_now)[None, :]
        scores = jnp.where(causal[None], scores, -1e+30)
        row_max = lax.optimization_barrier(jnp.max(scores, axis=-1, keepdims=True))
        weights = jnp.exp(scores - row_max)
        weights = weights / lax.optimization_barrier(jnp.sum(weights, axis=-1, keepdims=True))
        return jnp.einsum('hts,shd->thd', weights, values_in, precision=lax.Precision.HIGHEST)
    return lax.cond(kind == 1, attend, recurrent, projected)

def layer_backward(x_block, grad_y, w_in_l, w_out_l, gain_l, rate_l, kind):
    x_float = x_block.astype(jnp.float32)
    recip = lax.rsqrt(lax.optimization_barrier(jnp.mean(x_float * x_float, axis=-1, keepdims=True)) + EPSILON)
    gain_f = gain_l.astype(jnp.float32)
    normed = (x_float * recip * gain_f).astype(jnp.bfloat16)
    projected = jnp.dot(normed, w_in_l, preferred_element_type=jnp.float32)
    heads = projected.shape[1] // HEAD
    shaped = projected.reshape(TOK, heads, HEAD)
    rates = rate_l.astype(jnp.float32).reshape(heads, HEAD)
    mixed, mix_pull = jax.vjp(lambda values_in: mix_channels(values_in, rates, kind), shaped)
    mixed_b = mixed.reshape(TOK, heads * HEAD).astype(jnp.bfloat16)
    grad_mixed = jnp.dot(grad_y, w_out_l.T, preferred_element_type=jnp.float32)
    grad_w_out = jnp.dot(mixed_b.T, grad_y, preferred_element_type=jnp.float32)
    grad_proj = mix_pull(grad_mixed.reshape(TOK, heads, HEAD))[0].reshape(TOK, heads * HEAD).astype(jnp.bfloat16)
    grad_w_in = jnp.dot(normed.T, grad_proj, preferred_element_type=jnp.float32)

    def add_head(head_index, total_sum):
        first_col = (head_index * HEAD).astype(jnp.int32)
        columns = lax.dynamic_slice_in_dim(grad_proj, first_col, HEAD, 1)
        weight_cols = lax.dynamic_slice_in_dim(w_in_l, first_col, HEAD, 1)
        term = lax.dot_general(columns, weight_cols, (((1,), (1,)), ((), ())), preferred_element_type=jnp.float32)
        rounded = lax.optimization_barrier(term.astype(jnp.bfloat16))
        return total_sum + rounded.astype(jnp.float32)
    grad_normed = lax.fori_loop(0, heads, add_head, jnp.zeros((TOK, x_block.shape[1]), jnp.float32))
    scaled = grad_normed * gain_f
    grad_x = recip * scaled - x_float * recip ** 3 * lax.optimization_barrier(jnp.mean(scaled * x_float, axis=-1, keepdims=True))
    result = (grad_y.astype(jnp.float32) + grad_x).astype(jnp.bfloat16)
    return (result, grad_w_in, grad_w_out)

def reference(x_down, x_up, g_down, g_up, loss_grad, w_in, w_out, gain, retention, layer_kind):
    final_section = LAYERS - 1

    def run_layer(x_block, grad_y, layer):
        return layer_backward(x_block, grad_y, w_in[layer], w_out[layer], gain[layer], retention[layer], layer_kind[layer])
    indices = jnp.arange(LAYERS, dtype=jnp.int32)
    gx1_down = lax.map(lambda layer: run_layer(x_down[0, layer], g_down[layer], layer)[0], indices)
    gx1_up = lax.map(lambda device: run_layer(x_up[0, device], g_up[device], final_section - device)[0], indices)
    gy2_down = jnp.concatenate([gx1_down[1:], loss_grad[0:1]], axis=0)
    gy2_up = jnp.concatenate([loss_grad[1:2], gx1_up[:-1]], axis=0)

    def per_layer(layer):
        device_up = final_section - layer
        first_down = run_layer(x_down[0, layer], g_down[layer], layer)
        second_down = run_layer(x_down[1, layer], gy2_down[layer], layer)
        first_up = run_layer(x_up[0, device_up], g_up[device_up], layer)
        second_up = run_layer(x_up[1, device_up], gy2_up[device_up], layer)
        down_in = (first_down[1] + second_down[1]).astype(jnp.bfloat16).astype(jnp.float32)
        up_in = (first_up[1] + second_up[1]).astype(jnp.bfloat16).astype(jnp.float32)
        down_out = (first_down[2] + second_down[2]).astype(jnp.bfloat16).astype(jnp.float32)
        up_out = (first_up[2] + second_up[2]).astype(jnp.bfloat16).astype(jnp.float32)
        return (second_down[0], second_up[0], (down_in + up_in).astype(jnp.bfloat16), (down_out + up_out).astype(jnp.bfloat16))
    gx_down, gx_up_by_layer, grad_in, grad_out = lax.map(per_layer, indices)
    gx_up = gx_up_by_layer[::-1]
    return (gx_down, gx_up, grad_in, grad_out)
```

```python
import functools

import jax
import jax.numpy as jnp
from jax import lax
from jax.experimental import pallas as pl
from jax.experimental.pallas import tpu as pltpu
from jax.sharding import PartitionSpec as P

EPSILON = 1e-05
XN = 4
YN = 4
MESH = pl.DeviceIdType.MESH
F32 = jnp.float32
BF16 = jnp.bfloat16
HIGHEST = lax.Precision.HIGHEST

AG_SEMS = 24
RS_SEMS = 32


def kernel(
    sections, x_down, x_up, g_down, g_up, loss_grad, w_in, w_out, gain, retention, layer_kind,
    out_down, out_up, out_in, out_out,
    mirror_x, mirror_g, xs, gs, gat, gps, csend, crecv, part, xrelay, xfrom, yacc, yrelay, yfrom,
    hop_send, hop_recv, back_send, back_recv, send_sem, recv_sem,
):
    half = w_in.shape[0] // 2
    s = lax.axis_index("section")
    t = lax.axis_index("tensor")
    core = lax.rem(t, 2)
    y = lax.rem(t // 2, YN)
    x = t // (2 * YN)
    xr, xl, xo = lax.rem(x + 1, XN), lax.rem(x + 3, XN), lax.rem(x + 2, XN)
    yr, yl, yo = lax.rem(y + 1, YN), lax.rem(y + 3, YN), lax.rem(y + 2, YN)

    def tensor_id(xx, yy, cc):
        return (xx * YN + yy) * 2 + cc

    to_xr = (s, tensor_id(xr, y, core))
    to_xl = (s, tensor_id(xl, y, core))
    to_yr = (s, tensor_id(x, yr, core))
    to_yl = (s, tensor_id(x, yl, core))
    to_core = (s, tensor_id(x, y, 1 - core))
    to_mirror = (sections - 1 - s, t)
    to_next = (lax.rem(s + sections - 1, sections), t)
    to_prev = (lax.rem(s + 1, sections), t)

    barrier = pltpu.get_barrier_semaphore()
    peers = (to_xr, to_xl, to_yr, to_yl, to_core, to_mirror, to_next, to_prev)
    for peer in peers:
        pl.semaphore_signal(barrier, inc=1, device_id=peer, device_id_type=MESH)
    pl.semaphore_wait(barrier, len(peers))

    sent = []
    count = [0]

    def send(src, dst, device):
        index = count[0]
        count[0] += 1
        copy = pltpu.make_async_remote_copy(
            src_ref=src, dst_ref=dst, send_sem=send_sem.at[index], recv_sem=recv_sem.at[index],
            device_id=device, device_id_type=MESH,
        )
        copy.start()
        sent.append(copy)
        return copy

    mx = send(x_up, mirror_x, to_mirror)
    mg = send(g_up, mirror_g, to_mirror)

    gain_f = gain[...].astype(F32)
    rates = retention[...].astype(F32)
    lane_kind = lax.broadcasted_iota(jnp.int32, layer_kind.shape, 1)
    kind = jnp.sum(jnp.where(lane_kind == s, layer_kind[...], 0), axis=1, keepdims=True)
    is_attention = kind == 1

    def recip_of(rows):
        return lax.rsqrt(jnp.mean(rows * rows, axis=-1, keepdims=True) + EPSILON)

    def put_unit(index, rows):
        for h in range(2):
            gat[index, h, core, x, y] = rows[:, h * half:(h + 1) * half]

    for tick in range(2):
        xs[tick, 0:4, :] = x_down[tick].astype(F32)
    gs[0, 0:4, :] = g_down[...].astype(F32)
    mx.wait_recv()
    for tick in range(2):
        xs[tick, 4:8, :] = mirror_x[tick].astype(F32)
    mg.wait_recv()
    gs[0, 4:8, :] = mirror_g[...].astype(F32)
    put_unit(1, gs[0].astype(BF16))
    for tick in range(2):
        rows = xs[tick]
        put_unit(2 * tick, (rows * recip_of(rows) * gain_f).astype(BF16))

    def gather(first, number):
        sets = pl.ds(first, number)

        def unit(xx, yy, h=None):
            if h is None:
                return gat.at[sets, :, core, xx, yy]
            return gat.at[sets, h, core, xx, yy]

        def both(xx, yy):
            ref = unit(xx, yy)
            return send(ref, ref, to_xr), send(ref, ref, to_xl)

        def across(xx):
            ref = gat.at[sets, :, core, xx]
            return send(ref, ref, to_core)

        own = unit(x, y)
        from_yl, from_yr = send(own, own, to_yr), send(own, own, to_yl)
        x_sends = [both(x, y)]
        yield
        from_yl.wait_recv()
        ref = unit(x, yl, 0)
        relay_r = send(ref, ref, to_yr)
        from_yr.wait_recv()
        ref = unit(x, yr, 1)
        relay_l = send(ref, ref, to_yl)
        x_sends.append(both(x, yl))
        x_sends.append(both(x, yr))
        yield
        relays = []

        def relay_x(k, yy):
            from_xl, from_xr = x_sends[k]
            from_xl.wait_recv()
            ref = unit(xl, yy, 0)
            right = send(ref, ref, to_xr)
            from_xr.wait_recv()
            ref = unit(xr, yy, 1)
            relays.append((right, send(ref, ref, to_xl)))

        relay_x(0, y)
        relay_r.wait_recv()
        relay_l.wait_recv()
        x_sends.append(both(x, yo))
        crossing = [across(x)]
        yield
        relay_x(1, yl)
        relay_x(2, yr)
        yield
        relay_x(3, yo)
        crossing.append(across(xl))
        crossing.append(across(xr))
        yield
        for right, left in relays:
            right.wait_recv()
            left.wait_recv()
        crossing.append(across(xo))
        yield
        for copy in crossing:
            copy.wait_recv()

    def finish(steps):
        for _ in steps:
            pass

    def gathered(index, h):
        return gat[index, h].reshape(256, half)

    upper = lax.rem(lax.broadcasted_iota(jnp.int32, (128, 128), 0), 8) < 4

    def to_tokens(rows):
        first, second = rows[:128], rows[128:]
        down = jnp.where(upper, first, pltpu.roll(second, 4, 0))
        up = jnp.where(upper, pltpu.roll(first, 124, 0), second)
        return down, up

    def to_gathered(down, up):
        first = jnp.where(upper, down, pltpu.roll(up, 4, 0))
        second = jnp.where(upper, pltpu.roll(down, 124, 0), up)
        return first, second

    def projected_of(index):
        total = jnp.dot(gathered(index, 0), w_in[:half, :], preferred_element_type=F32)
        return total + jnp.dot(gathered(index, 1), w_in[half:, :], preferred_element_type=F32)

    def contract_last(left, right, **kw):
        return lax.dot_general(left, right, (((1,), (1,)), ((), ())), preferred_element_type=F32, **kw)

    def contract_first(left, right, **kw):
        return lax.dot_general(left, right, (((0,), (0,)), ((), ())), preferred_element_type=F32, **kw)

    def grad_mixed_of(index):
        total = contract_last(gathered(index, 0), w_out[:, :half])
        return total + contract_last(gathered(index, 1), w_out[:, half:])

    token = lax.broadcasted_iota(jnp.int32, (128, 256), 0)
    causal = lax.broadcasted_iota(jnp.int32, (128, 128), 0) >= lax.broadcasted_iota(jnp.int32, (128, 128), 1)
    low_lane = lax.broadcasted_iota(jnp.int32, (128, 128), 1) < 64
    rates2 = jnp.concatenate([rates, rates], axis=1)

    def scan(values, backward):
        state = values
        power = rates2
        step = 1
        while step < 128:
            if backward:
                moved = jnp.where(token < 128 - step, pltpu.roll(state, 128 - step, 0), 0.0)
            else:
                moved = jnp.where(token >= step, pltpu.roll(state, step, 0), 0.0)
            state = state + power * moved
            power = power * power
            step *= 2
        return state

    def mix_forward(pair):
        wide = jnp.concatenate(pair, axis=1)
        state = scan((1.0 - rates2) * wide, False)
        gate = jax.nn.sigmoid(wide)
        recurrent = state * (wide * gate)
        weights, mixed = [], []
        for d in range(2):
            v = pair[d]
            turned = pltpu.roll(v, 64, 1)
            scores = contract_last(jnp.where(low_lane, v, 0.0), turned, precision=HIGHEST) * 0.125
            scores = jnp.where(causal, scores, -1e30)
            w = jnp.exp(scores - jnp.max(scores, axis=-1, keepdims=True))
            w = w / jnp.sum(w, axis=-1, keepdims=True)
            attended = jnp.dot(w, v, precision=HIGHEST, preferred_element_type=F32)
            weights.append(w)
            mixed.append(jnp.where(is_attention, attended, recurrent[:, d * 128:(d + 1) * 128]))
        return mixed, (pair, wide, state, gate, weights)

    def mix_backward(saved, grads):
        pair, wide, state, gate, weights = saved
        g_wide = jnp.concatenate(grads, axis=1)
        d_state = scan(g_wide * (wide * gate), True)
        recurrent = (1.0 - rates2) * d_state + g_wide * state * (gate * (1.0 + wide * (1.0 - gate)))
        result = []
        for d in range(2):
            v, g, w = pair[d], grads[d], weights[d]
            turned = pltpu.roll(v, 64, 1)
            d_weights = contract_last(g, v, precision=HIGHEST)
            d_scores = w * (d_weights - jnp.sum(w * d_weights, axis=-1, keepdims=True)) * 0.125
            d_query = jnp.dot(d_scores, turned, precision=HIGHEST, preferred_element_type=F32)
            d_key = contract_first(d_scores, v, precision=HIGHEST)
            attended = contract_first(w, g, precision=HIGHEST) + jnp.where(
                low_lane, d_query, pltpu.roll(d_key, 64, 1)
            )
            result.append(jnp.where(is_attention, attended, recurrent[:, d * 128:(d + 1) * 128]))
        return result

    y_order = (yo, yr, yl, y)

    def add(*pieces):
        total = pieces[0].astype(F32)
        for piece in pieces[1:]:
            total = total + piece.astype(F32)
        return total

    def scatter(tick):
        def terms(which, h):
            weights = w_in[h * half:(h + 1) * half, :]
            return contract_last(gps[tick, which], weights).astype(BF16).reshape(XN, YN, 8, half)

        crossing = []
        for h in range(2):
            csend[tick, h] = terms(1 - core, h)
            crossing.append(send(csend.at[tick, h], crecv.at[tick, h], to_core))
        yield
        for h in range(2):
            own = terms(core, h)
            crossing[h].wait_recv()
            part[tick, h] = add(own, crecv[tick, h]).astype(BF16)
        first, plain, joined = [], [], []
        p, xy, xf = part.at[tick], xrelay.at[tick], xfrom.at[tick]
        for yy in y_order:
            first.append((
                send(p.at[0, xo, yy], xy.at[0, yy], to_xr),
                send(p.at[1, xo, yy], xy.at[1, yy], to_xl),
            ))
        for yy in y_order:
            plain.append((
                send(p.at[1, xr, yy], xf.at[0, 1, yy], to_xr),
                send(p.at[0, xl, yy], xf.at[1, 0, yy], to_xl),
            ))
        yield
        for k, yy in enumerate(y_order):
            first[k][0].wait_recv()
            part[tick, 0, xr, yy] = add(part[tick, 0, xr, yy], xrelay[tick, 0, yy]).astype(BF16)
            right = send(p.at[0, xr, yy], xf.at[0, 0, yy], to_xr)
            first[k][1].wait_recv()
            part[tick, 1, xl, yy] = add(part[tick, 1, xl, yy], xrelay[tick, 1, yy]).astype(BF16)
            joined.append((right, send(p.at[1, xl, yy], xf.at[1, 1, yy], to_xl)))
            if k % 2 == 1:
                yield

        def reduce_x(k):
            yy = y_order[k]
            for copy in plain[k] + joined[k]:
                copy.wait_recv()
            for h in range(2):
                yacc[tick, h, yy] = add(
                    part[tick, h, x, yy], xfrom[tick, 0, h, yy], xfrom[tick, 1, h, yy]
                ).astype(BF16)

        q, yrl, yf = yacc.at[tick], yrelay.at[tick], yfrom.at[tick]
        reduce_x(0)
        first_r = send(q.at[0, yo], yrl.at[0], to_yr)
        first_l = send(q.at[1, yo], yrl.at[1], to_yl)
        reduce_x(1)
        plain_r = send(q.at[1, yr], yf.at[0, 1], to_yr)
        reduce_x(2)
        plain_l = send(q.at[0, yl], yf.at[1, 0], to_yl)
        yield
        first_r.wait_recv()
        yacc[tick, 0, yr] = add(yacc[tick, 0, yr], yrelay[tick, 0]).astype(BF16)
        joined_r = send(q.at[0, yr], yf.at[0, 0], to_yr)
        first_l.wait_recv()
        yacc[tick, 1, yl] = add(yacc[tick, 1, yl], yrelay[tick, 1]).astype(BF16)
        joined_l = send(q.at[1, yl], yf.at[1, 1], to_yl)
        yield
        reduce_x(3)
        for copy in (plain_r, plain_l, joined_r, joined_l):
            copy.wait_recv()
        halves = [
            add(yacc[tick, h, y], yfrom[tick, 0, h], yfrom[tick, 1, h]) for h in range(2)
        ]
        rows = xs[tick]
        recip = recip_of(rows)
        scaled = jnp.concatenate(halves, axis=1) * gain_f
        along = jnp.mean(scaled * rows, axis=-1, keepdims=True)
        xs[tick] = gs[tick] + (recip * scaled - rows * (recip * recip * recip) * along)

    gather_1 = gather(0, 2)
    for _ in range(6):
        next(gather_1)
    gather_2 = gather(2, 1)
    next(gather_2)
    finish(gather_1)

    def split_rows(pair):
        first, second = to_gathered(*pair)
        return first, second

    def spread(first, second):
        rows = jnp.concatenate([first, second], axis=0)
        mask = lax.rem(lax.broadcasted_iota(jnp.int32, (256, 128), 0), 8) < 4
        return jnp.concatenate([jnp.where(mask, rows, 0.0), jnp.where(mask, 0.0, rows)], axis=1)

    pair_1 = to_tokens(projected_of(0))
    grads_1 = to_tokens(grad_mixed_of(1))
    next(gather_2)
    mixed_1, saved_1 = mix_forward(pair_1)
    d_pair = mix_backward(saved_1, grads_1)
    next(gather_2)
    first, second = split_rows(d_pair)
    gps[0, 0] = first.astype(BF16)
    gps[0, 1] = second.astype(BF16)
    gp_wide_1 = spread(first, second).astype(BF16)
    mixed_wide_1 = spread(*split_rows(mixed_1)).astype(BF16)
    scatter_1 = scatter(0)
    next(scatter_1)
    next(gather_2)
    next(scatter_1)
    next(gather_2)
    next(scatter_1)
    next(gather_2)
    next(scatter_1)
    finish(gather_2)
    pair_2 = to_tokens(projected_of(2))
    next(scatter_1)
    next(scatter_1)
    finish(scatter_1)
    hop_send[...] = xs[0].astype(BF16)
    hop = send(hop_send, hop_recv, to_next)
    mixed_2, saved_2 = mix_forward(pair_2)
    mixed_wide_2 = spread(*split_rows(mixed_2)).astype(BF16)
    hop.wait_recv()
    gs[1, 0:4, :] = loss_grad[0].astype(F32)
    gs[1, 4:8, :] = loss_grad[1].astype(F32)
    gs[1] = jnp.where(s == sections - 1, gs[1], hop_recv[...].astype(F32))
    put_unit(3, gs[1].astype(BF16))
    finish(gather(3, 1))
    grads_2 = to_tokens(grad_mixed_of(3))
    first, second = split_rows(mix_backward(saved_2, grads_2))
    gps[1, 0] = first.astype(BF16)
    gps[1, 1] = second.astype(BF16)
    gp_wide_2 = spread(first, second).astype(BF16)
    scatter_2 = scatter(1)
    next(scatter_2)
    next(scatter_2)

    block = 256
    per_half = half // block
    gp_both = jnp.concatenate([gp_wide_1, gp_wide_2], axis=0)
    mixed_both = jnp.concatenate([mixed_wide_1, mixed_wide_2], axis=0)

    def columns(index, h, at):
        return gat[index, h, :, :, :, :, pl.ds(at, block)].reshape(256, block)

    def weight_in(h):
        def step(i, _):
            at = pl.multiple_of(i * block, block)
            left = jnp.concatenate([columns(0, h, at), columns(2, h, at)], axis=0)
            total = contract_first(left, gp_both)
            down = total[:, :128].astype(BF16).astype(F32)
            up = total[:, 128:].astype(BF16).astype(F32)
            out_in[pl.ds(h * half + at, block), :] = (down + up).astype(BF16)
            return 0

        lax.fori_loop(0, per_half, step, 0)

    def weight_out(h):
        def step(i, _):
            at = pl.multiple_of(i * block, block)
            right = jnp.concatenate([columns(1, h, at), columns(3, h, at)], axis=0)
            total = contract_first(mixed_both, right)
            down = total[:128].astype(BF16).astype(F32)
            up = total[128:].astype(BF16).astype(F32)
            out_out[:, pl.ds(h * half + at, block)] = (down + up).astype(BF16)
            return 0

        lax.fori_loop(0, per_half, step, 0)

    weight_out(0)
    next(scatter_2)
    weight_out(1)
    next(scatter_2)
    weight_in(0)
    next(scatter_2)
    next(scatter_2)
    finish(scatter_2)
    back_send[...] = xs[1, 4:8, :].astype(BF16)
    back = send(back_send, back_recv, to_mirror)
    out_down[...] = xs[1, 0:4, :].astype(BF16)
    weight_in(1)
    back.wait_recv()
    out_up[...] = back_recv[...]
    for copy in sent:
        copy.wait_send()


def body(x_down, x_up, g_down, g_up, loss_grad, w_in, w_out, gain, retention, layer_kind):
    sections = lax.axis_size("section")
    width = w_in.shape[1]
    half = width // 2
    vmem = pl.BlockSpec(memory_space=pltpu.VMEM)
    copies = 3 * AG_SEMS + 2 * RS_SEMS + 4
    down, up, grad_in, grad_out = pl.pallas_call(
        functools.partial(kernel, sections),
        out_shape=(
            jax.ShapeDtypeStruct((4, width), BF16),
            jax.ShapeDtypeStruct((4, width), BF16),
            jax.ShapeDtypeStruct((width, 128), BF16),
            jax.ShapeDtypeStruct((128, width), BF16),
        ),
        in_specs=[vmem] * 10,
        out_specs=(vmem,) * 4,
        scratch_shapes=[
            pltpu.VMEM((2, 4, width), BF16),
            pltpu.VMEM((4, width), BF16),
            pltpu.VMEM((2, 8, width), F32),
            pltpu.VMEM((2, 8, width), F32),
            pltpu.VMEM((4, 2, 2, XN, YN, 8, half), BF16),
            pltpu.VMEM((2, 2, 128, 128), BF16),
            pltpu.VMEM((2, 2, XN, YN, 8, half), BF16),
            pltpu.VMEM((2, 2, XN, YN, 8, half), BF16),
            pltpu.VMEM((2, 2, XN, YN, 8, half), BF16),
            pltpu.VMEM((2, 2, YN, 8, half), BF16),
            pltpu.VMEM((2, 2, 2, YN, 8, half), BF16),
            pltpu.VMEM((2, 2, YN, 8, half), BF16),
            pltpu.VMEM((2, 2, 8, half), BF16),
            pltpu.VMEM((2, 2, 2, 8, half), BF16),
            pltpu.VMEM((8, width), BF16),
            pltpu.VMEM((8, width), BF16),
            pltpu.VMEM((4, width), BF16),
            pltpu.VMEM((4, width), BF16),
            pltpu.SemaphoreType.DMA((copies,)),
            pltpu.SemaphoreType.DMA((copies,)),
        ],
        compiler_params=pltpu.CompilerParams(
            collective_id=0, has_side_effects=True, vmem_limit_bytes=56 * 1024 * 1024
        ),
    )(
        x_down[:, 0], x_up[:, 0], g_down[0], g_up[0], loss_grad, w_in[0], w_out[0], gain, retention,
        layer_kind.reshape(1, -1),
    )
    return (down[None], up[None], grad_in[None], grad_out[None])


def solution(mesh):
    return jax.shard_map(
        body,
        mesh=mesh,
        in_specs=(
            P(None, "section", "tensor", None),
            P(None, "section", "tensor", None),
            P("section", "tensor", None),
            P("section", "tensor", None),
            P(None, "tensor", None),
            P("section", None, "tensor"),
            P("section", "tensor", None),
            P("section", None),
            P("section", "tensor"),
            P(),
        ),
        out_specs=(
            P("section", "tensor", None),
            P("section", "tensor", None),
            P("section", None, "tensor"),
            P("section", "tensor", None),
        ),
        check_vma=False,
    )
```

```python
import functools

import jax
import jax.numpy as jnp
from jax import lax
from jax.experimental import pallas as pl
from jax.experimental.pallas import tpu as pltpu
from jax.sharding import PartitionSpec as P

EPSILON = 1e-05
XN = 4
YN = 4
Y_DIRECT = False
X_DIRECT = False
SHARED_AT = 3
MESH = pl.DeviceIdType.MESH
F32 = jnp.float32
BF16 = jnp.bfloat16
HIGHEST = lax.Precision.HIGHEST

AG_SEMS = 24
RS_SEMS = 32


def kernel(
    sections, x_down_h, x_up_h, g_down_h, g_up_h, loss_h, w_in_h, w_out_h, gain_h, retention_h, kind_h,
    down_h, up_h, in_h, out_h,
    x_rows, g_rows, loss_rows, w_in, w_out, gain, retention, layer_kind, out_down, back_send, back_recv,
    out_in, out_out, load_sem, store_sem,
    xs, gs, gat, csend, crecv, part, xrelay, xfrom, yacc, yrelay, yfrom,
    pre_send, pre_recv, fin_send, fin_recv, hop_send, hop_recv, side_send, side_recv,
    send_sem, recv_sem,
):
    width = w_in.shape[0]
    half = width // 2
    quarter = width // 4
    loads = [
        pltpu.make_async_copy(src, dst, load_sem.at[i])
        for i, (src, dst) in enumerate((
            (x_down_h, x_rows.at[0]), (g_down_h, g_rows.at[0]), (gain_h, gain), (loss_h, loss_rows),
            (retention_h, retention), (kind_h, layer_kind), (w_in_h, w_in), (w_out_h, w_out),
        ))
    ]
    for copy in loads:
        copy.start()
    s = lax.axis_index("section")
    t = lax.axis_index("tensor")
    core = lax.rem(t, 2)
    y = lax.rem(t // 2, YN)
    x = t // (2 * YN)
    xr, xl, xo = lax.rem(x + 1, XN), lax.rem(x + 3, XN), lax.rem(x + 2, XN)
    yr, yl, yo = lax.rem(y + 1, YN), lax.rem(y + 3, YN), lax.rem(y + 2, YN)

    def tensor_id(xx, yy, cc):
        return (xx * YN + yy) * 2 + cc

    next_section = lax.rem(s + sections - 1, sections)
    prev_section = lax.rem(s + 1, sections)
    other = tensor_id(x, y, 1 - core)
    to_xr = (s, tensor_id(xr, y, core))
    to_xl = (s, tensor_id(xl, y, core))
    to_yr = (s, tensor_id(x, yr, core))
    to_yl = (s, tensor_id(x, yl, core))
    to_xo = (s, tensor_id(xo, y, core))
    to_yo = (s, tensor_id(x, yo, core))
    to_core = (s, other)
    to_mirror = (sections - 1 - s, t)
    to_next, to_next_side = (next_section, t), (next_section, other)
    to_prev, to_prev_side = (prev_section, t), (prev_section, other)

    barrier = pltpu.get_barrier_semaphore()
    peers = [
        to_xr, to_xl, to_yr, to_yl, to_core, to_mirror, to_next, to_prev, to_next_side, to_prev_side,
    ]
    if Y_DIRECT:
        peers.append(to_yo)
    if X_DIRECT:
        peers.append(to_xo)
    for peer in peers:
        pl.semaphore_signal(barrier, inc=1, device_id=peer, device_id_type=MESH)
    pl.semaphore_wait(barrier, len(peers))

    sent = []

    def send(src, dst, device):
        index = len(sent)
        copy = pltpu.make_async_remote_copy(
            src_ref=src, dst_ref=dst, send_sem=send_sem.at[index], recv_sem=recv_sem.at[index],
            device_id=device, device_id_type=MESH,
        )
        copy.start()
        sent.append(copy)
        return copy

    stores = []

    def store(src, dst):
        copy = pltpu.make_async_copy(src, dst, store_sem.at[len(stores)])
        copy.start()
        stores.append(copy)

    mx = send(x_up_h, x_rows.at[1], to_mirror)
    mg = send(g_up_h, g_rows.at[1], to_mirror)
    for copy in loads[:6]:
        copy.wait()

    gain_f = gain[...].astype(F32)
    rates = retention[...].astype(F32)
    lane_kind = lax.broadcasted_iota(jnp.int32, layer_kind.shape, 1)
    kind = jnp.sum(jnp.where(lane_kind == s, layer_kind[...], 0), axis=1, keepdims=True)
    is_attention = kind == 1
    first_core = core == 0

    def recip_of(rows):
        return lax.rsqrt(jnp.mean(rows * rows, axis=-1, keepdims=True) + EPSILON)

    def mine(rows):
        return jnp.where(first_core, rows[:, :half], rows[:, half:])

    def theirs(rows):
        return jnp.where(first_core, rows[:, half:], rows[:, :half])

    def put_unit(d, index, own, received):
        first = jnp.where(first_core, own, received)
        second = jnp.where(first_core, received, own)
        unit = jnp.concatenate([first, second], axis=0).astype(BF16)
        for q in range(2):
            gat[d, index, core, q, x, y] = unit[:, q * quarter:(q + 1) * quarter]

    def prepare(d):
        kept = []
        for tick in range(2):
            rows = x_rows[d, tick].astype(F32)
            xs[d, tick] = rows
            normed = (rows * recip_of(rows) * gain_f).astype(BF16).astype(F32)
            pre_send[d, 2 * tick] = theirs(normed).astype(BF16)
            kept.append(mine(normed))
        grads = g_rows[d].astype(F32)
        gs[d, 0] = grads
        pre_send[d, 1] = theirs(grads).astype(BF16)
        pre_send[d, 3] = theirs(loss_rows[d].astype(F32)).astype(BF16)
        copy = send(pre_send.at[d], pre_recv.at[d], to_core)
        copy.wait_recv()
        put_unit(d, 0, kept[0], pre_recv[d, 0].astype(F32))
        put_unit(d, 1, mine(grads), pre_recv[d, 1].astype(F32))
        put_unit(d, 2, kept[1], pre_recv[d, 2].astype(F32))

    def gather(directions, sets):
        def unit(xx, yy, q=None):
            if q is None:
                return gat.at[directions, sets, core, :, xx, yy]
            return gat.at[directions, sets, core, q, xx, yy]

        def spread_x(yy):
            ref = unit(x, yy)
            copies = [send(ref, ref, to_xr), send(ref, ref, to_xl)]
            if X_DIRECT:
                copies.append(send(ref, ref, to_xo))
            return copies

        def across(xx):
            ref = gat.at[directions, sets, core, :, xx]
            return send(ref, ref, to_core)

        own = unit(x, y)
        from_yl, from_yr = send(own, own, to_yr), send(own, own, to_yl)
        if Y_DIRECT:
            from_yo = [send(own, own, to_yo)]
        x_sends = [spread_x(y)]
        yield
        from_yl.wait_recv()
        if not Y_DIRECT:
            ref = unit(x, yl, 0)
            from_yo = [send(ref, ref, to_yr)]
        x_sends.append(spread_x(yl))
        from_yr.wait_recv()
        if not Y_DIRECT:
            ref = unit(x, yr, 1)
            from_yo.append(send(ref, ref, to_yl))
        x_sends.append(spread_x(yr))
        yield
        relays = []

        def relay_x(k, yy):
            x_sends[k][0].wait_recv()
            if not X_DIRECT:
                ref = unit(xl, yy, 0)
                relays.append(send(ref, ref, to_xr))
            x_sends[k][1].wait_recv()
            if not X_DIRECT:
                ref = unit(xr, yy, 1)
                relays.append(send(ref, ref, to_xl))

        if not Y_DIRECT:
            relay_x(0, y)
        for copy in from_yo:
            copy.wait_recv()
        x_sends.append(spread_x(yo))
        if Y_DIRECT:
            relay_x(0, y)
        crossing = [across(x)]
        yield
        relay_x(1, yl)
        relay_x(2, yr)
        yield
        relay_x(3, yo)
        crossing.append(across(xl))
        crossing.append(across(xr))
        yield
        for copy in relays:
            copy.wait_recv()
        if X_DIRECT:
            for copies in x_sends:
                copies[2].wait_recv()
        crossing.append(across(xo))
        yield
        for copy in crossing:
            copy.wait_recv()

    def gathered(d, index, i):
        return gat[d, index, i // 2, i % 2].reshape(128, quarter)

    def contract_last(left, right, **kw):
        return lax.dot_general(left, right, (((1,), (1,)), ((), ())), preferred_element_type=F32, **kw)

    def contract_first(left, right, **kw):
        return lax.dot_general(left, right, (((0,), (0,)), ((), ())), preferred_element_type=F32, **kw)

    def projected_of(d, index):
        total = 0.0
        for i in range(4):
            total = total + jnp.dot(
                gathered(d, index, i), w_in[i * quarter:(i + 1) * quarter, :], preferred_element_type=F32
            )
        return total

    def grad_mixed_of(d, index):
        total = 0.0
        for i in range(4):
            total = total + contract_last(gathered(d, index, i), w_out[:, i * quarter:(i + 1) * quarter])
        return total

    token = lax.broadcasted_iota(jnp.int32, (128, 128), 0)
    lane = lax.broadcasted_iota(jnp.int32, (128, 128), 1)
    causal = token >= lane
    low_lane = lane < 64

    def scan(values, backward):
        state = values
        power = rates
        step = 1
        while step < 128:
            if backward:
                moved = jnp.where(token < 128 - step, pltpu.roll(state, 128 - step, 0), 0.0)
            else:
                moved = jnp.where(token >= step, pltpu.roll(state, step, 0), 0.0)
            state = state + power * moved
            power = power * power
            step *= 2
        return state

    def mix_forward(v):
        state = scan((1.0 - rates) * v, False)
        gate = jax.nn.sigmoid(v)
        recurrent = state * (v * gate)
        turned = pltpu.roll(v, 64, 1)
        scores = contract_last(jnp.where(low_lane, v, 0.0), turned, precision=HIGHEST) * 0.125
        scores = jnp.where(causal, scores, -1e30)
        weights = jnp.exp(scores - jnp.max(scores, axis=-1, keepdims=True))
        weights = weights / jnp.sum(weights, axis=-1, keepdims=True)
        attended = jnp.dot(weights, v, precision=HIGHEST, preferred_element_type=F32)
        mixed = jnp.where(is_attention, attended, recurrent)
        return mixed.astype(BF16), (v, state, gate, weights)

    def mix_backward(saved, g):
        v, state, gate, weights = saved
        d_state = scan(g * (v * gate), True)
        recurrent = (1.0 - rates) * d_state + g * state * (gate * (1.0 + v * (1.0 - gate)))
        turned = pltpu.roll(v, 64, 1)
        d_weights = contract_last(g, v, precision=HIGHEST)
        d_scores = weights * (d_weights - jnp.sum(weights * d_weights, axis=-1, keepdims=True)) * 0.125
        d_query = jnp.dot(d_scores, turned, precision=HIGHEST, preferred_element_type=F32)
        d_key = contract_first(d_scores, v, precision=HIGHEST)
        attended = contract_first(weights, g, precision=HIGHEST) + jnp.where(
            low_lane, d_query, pltpu.roll(d_key, 64, 1)
        )
        return jnp.where(is_attention, attended, recurrent).astype(BF16)

    y_order = (yo, yr, yl, y)

    def add(*pieces):
        total = pieces[0].astype(F32)
        for piece in pieces[1:]:
            total = total + piece.astype(F32)
        return total

    def scatter(d, tick, grad_proj):
        def terms(which, q):
            at = pl.multiple_of(which * half + q * quarter, quarter)
            weights = w_in[pl.ds(at, quarter), :]
            return contract_last(grad_proj, weights).astype(BF16).reshape(XN, YN, 8, quarter)

        crossing = []
        for q in range(2):
            csend[d, tick, q] = terms(1 - core, q)
            crossing.append(send(csend.at[d, tick, q], crecv.at[d, tick, q], to_core))
        own = [terms(core, q) for q in range(2)]
        yield
        for q in range(2):
            crossing[q].wait_recv()
            part[d, tick, q] = add(own[q], crecv[d, tick, q]).astype(BF16)
        first, plain, joined = [], [], []
        p, xy, xf = part.at[d, tick], xrelay.at[d, tick], xfrom.at[d, tick]
        if X_DIRECT:
            for yy in y_order:
                plain.append([
                    send(p.at[:, xo, yy], xf.at[2, :, yy], to_xo),
                    send(p.at[:, xr, yy], xf.at[0, :, yy], to_xr),
                    send(p.at[:, xl, yy], xf.at[1, :, yy], to_xl),
                ])
                joined.append([])
            yield
        else:
            for yy in y_order:
                first.append((
                    send(p.at[0, xo, yy], xy.at[0, yy], to_xr),
                    send(p.at[1, xo, yy], xy.at[1, yy], to_xl),
                ))
                plain.append([
                    send(p.at[1, xr, yy], xf.at[0, 1, yy], to_xr),
                    send(p.at[0, xl, yy], xf.at[1, 0, yy], to_xl),
                ])
            yield
            for k, yy in enumerate(y_order):
                first[k][0].wait_recv()
                part[d, tick, 0, xr, yy] = add(part[d, tick, 0, xr, yy], xrelay[d, tick, 0, yy]).astype(BF16)
                right = send(p.at[0, xr, yy], xf.at[0, 0, yy], to_xr)
                first[k][1].wait_recv()
                part[d, tick, 1, xl, yy] = add(part[d, tick, 1, xl, yy], xrelay[d, tick, 1, yy]).astype(BF16)
                joined.append([right, send(p.at[1, xl, yy], xf.at[1, 1, yy], to_xl)])
                if k % 2 == 1:
                    yield

        def reduce_x(k):
            yy = y_order[k]
            for copy in plain[k] + joined[k]:
                copy.wait_recv()
            for q in range(2):
                pieces = [xfrom[d, tick, i, q, yy] for i in range(3 if X_DIRECT else 2)]
                yacc[d, tick, q, yy] = add(part[d, tick, q, x, yy], *pieces).astype(BF16)

        a, yrl, yf = yacc.at[d, tick], yrelay.at[d, tick], yfrom.at[d, tick]
        reduce_x(0)
        if Y_DIRECT:
            last = [send(a.at[:, yo], yf.at[2], to_yo)]
            reduce_x(1)
            last.append(send(a.at[:, yr], yf.at[0], to_yr))
            reduce_x(2)
            last.append(send(a.at[:, yl], yf.at[1], to_yl))
            reduce_x(3)
            yield
        else:
            first_r = send(a.at[0, yo], yrl.at[0], to_yr)
            first_l = send(a.at[1, yo], yrl.at[1], to_yl)
            reduce_x(1)
            last = [send(a.at[1, yr], yf.at[0, 1], to_yr)]
            reduce_x(2)
            last.append(send(a.at[0, yl], yf.at[1, 0], to_yl))
            reduce_x(3)
            yield
            first_r.wait_recv()
            yacc[d, tick, 0, yr] = add(yacc[d, tick, 0, yr], yrelay[d, tick, 0]).astype(BF16)
            last.append(send(a.at[0, yr], yf.at[0, 0], to_yr))
            first_l.wait_recv()
            yacc[d, tick, 1, yl] = add(yacc[d, tick, 1, yl], yrelay[d, tick, 1]).astype(BF16)
            last.append(send(a.at[1, yl], yf.at[1, 1], to_yl))
            yield
        for copy in last:
            copy.wait_recv()
        summed = jnp.concatenate([
            add(yacc[d, tick, q, y], *[yfrom[d, tick, i, q] for i in range(3 if Y_DIRECT else 2)])
            for q in range(2)
        ], axis=1)
        fin_send[d, tick] = jnp.where(first_core, summed[4:], summed[:4])
        swap = send(fin_send.at[d, tick], fin_recv.at[d, tick], to_core)
        kept = jnp.where(first_core, summed[:4], summed[4:])
        rows = xs[d, tick]
        recip = recip_of(rows)
        swap.wait_recv()
        received = fin_recv[d, tick]
        scaled = jnp.concatenate([
            jnp.where(first_core, kept, received), jnp.where(first_core, received, kept)
        ], axis=1) * gain_f
        along = jnp.mean(scaled * rows, axis=-1, keepdims=True)
        xs[d, tick] = gs[d, tick] + (recip * scaled - rows * (recip * recip * recip) * along)

    block = min(256, quarter)
    per_quarter = quarter // block

    def columns(d, index, i, at):
        return gat[d, index, i // 2, i % 2, :, :, :, pl.ds(at, block)].reshape(128, block)

    def both_ticks(d, index, i, at):
        return jnp.concatenate([columns(d, index, i, at), columns(d, index + 2, i, at)], axis=0)

    def weight_in(d, i, grad_both):
        def step(j, _):
            at = pl.multiple_of(j * block, block)
            rows = pl.ds(i * quarter + at, block)
            total = contract_first(both_ticks(d, 0, i, at), grad_both).astype(BF16)
            if d == 1:
                total = (out_in[rows, :].astype(F32) + total.astype(F32)).astype(BF16)
            out_in[rows, :] = total
            return 0

        lax.fori_loop(0, per_quarter, step, 0)

    def weight_out(d, i, mixed_turned):
        def step(j, _):
            at = pl.multiple_of(j * block, block)
            cols = pl.ds(i * quarter + at, block)
            total = jnp.dot(mixed_turned, both_ticks(d, 1, i, at), preferred_element_type=F32).astype(BF16)
            if d == 1:
                total = (out_out[:, cols].astype(F32) + total.astype(F32)).astype(BF16)
            out_out[:, cols] = total
            return 0

        lax.fori_loop(0, per_quarter, step, 0)

    def chain(d):
        one = pl.ds(d, 1)
        yield from gather(one, pl.ds(0, 2))
        if d == 0:
            loads[6].wait()
            loads[7].wait()
        mixed_1, saved = mix_forward(projected_of(d, 0))
        grad_proj_1 = mix_backward(saved, grad_mixed_of(d, 1))
        yield from scatter(d, 0, grad_proj_1)
        hop_send[d] = xs[d, 0].astype(BF16)
        side_send[d] = theirs(xs[d, 0]).astype(BF16)
        hop = send(hop_send.at[d], hop_recv.at[d], to_next)
        side = send(side_send.at[d], side_recv.at[d], to_next_side)
        yield "second"
        mixed_2, saved = mix_forward(projected_of(d, 2))
        mixed_turned = jnp.concatenate(
            [mixed_1.astype(F32), mixed_2.astype(F32)], axis=0
        ).T.astype(BF16)
        hop.wait_recv()
        side.wait_recv()
        at_top = s == sections - 1
        grads = jnp.where(at_top, loss_rows[d].astype(F32), hop_recv[d].astype(F32))
        gs[d, 1] = grads
        put_unit(
            d, 3, mine(grads),
            jnp.where(at_top, pre_recv[d, 3].astype(F32), side_recv[d].astype(F32)),
        )
        yield from gather(one, pl.ds(3, 1))
        grad_proj_2 = mix_backward(saved, grad_mixed_of(d, 3))
        steps = scatter(d, 1, grad_proj_2)
        grad_both = jnp.concatenate([grad_proj_1, grad_proj_2], axis=0)
        work = [functools.partial(weight_out, d, i, mixed_turned) for i in range(4)]
        work += [functools.partial(weight_in, d, i, grad_both) for i in range(4)]
        for _ in steps:
            yield
            if work:
                work.pop(0)()
        if d == 0:
            out_down[...] = xs[0, 1].astype(BF16)
            store(out_down, down_h)
        else:
            back_send[...] = xs[1, 1].astype(BF16)
            back = send(back_send, back_recv, to_mirror)
        while work:
            work.pop(0)()
        if d == 1:
            store(out_out, out_h)
            store(out_in, in_h)
            yield
            back.wait_recv()
            store(back_recv, up_h)

    prepare(0)
    down = chain(0)
    next(down)
    mx.wait_recv()
    mg.wait_recv()
    prepare(1)
    up = chain(1)
    shared = gather(pl.ds(0, 2), pl.ds(2, 1))
    turn = 0
    live = [down, up]
    while live:
        for steps in list(live):
            if next(steps, "end") == "second":
                for _ in shared:
                    pass
            if steps.gi_frame is None:
                live.remove(steps)
        turn += 1
        if turn >= SHARED_AT:
            next(shared, None)
    for copy in stores:
        copy.wait()
    for copy in sent:
        copy.wait_send()


def copy_out(*refs):
    sources, results, held, sem = refs[:4], refs[4:8], refs[8:12], refs[12]
    reads = [pltpu.make_async_copy(a, b, sem.at[0, i]) for i, (a, b) in enumerate(zip(sources, held))]
    writes = [pltpu.make_async_copy(a, b, sem.at[1, i]) for i, (a, b) in enumerate(zip(held, results))]
    for copy in reads:
        copy.start()
    for read, write in zip(reads, writes):
        read.wait()
        write.start()
    for copy in writes:
        copy.wait()


def body(x_down, x_up, g_down, g_up, loss_grad, w_in, w_out, gain, retention, layer_kind):
    sections = lax.axis_size("section")
    width = w_in.shape[1]
    half, quarter = width // 2, width // 4
    anywhere = pl.BlockSpec(memory_space=pl.ANY)
    copies = 5 * AG_SEMS + 4 * (RS_SEMS + 1) + 9
    results = pl.pallas_call(
        functools.partial(kernel, sections),
        out_shape=(
            jax.ShapeDtypeStruct((4, width), BF16),
            jax.ShapeDtypeStruct((4, width), BF16),
            jax.ShapeDtypeStruct((width, 128), BF16),
            jax.ShapeDtypeStruct((128, width), BF16),
        ),
        in_specs=[anywhere] * 10,
        out_specs=(anywhere,) * 4,
        scratch_shapes=[
            pltpu.VMEM((2, 2, 4, width), BF16),
            pltpu.VMEM((2, 4, width), BF16),
            pltpu.VMEM((2, 4, width), BF16),
            pltpu.VMEM((width, 128), BF16),
            pltpu.VMEM((128, width), BF16),
            pltpu.VMEM((1, width), BF16),
            pltpu.VMEM((1, 128), BF16),
            pltpu.VMEM((1, sections), jnp.int32),
            pltpu.VMEM((4, width), BF16),
            pltpu.VMEM((4, width), BF16),
            pltpu.VMEM((4, width), BF16),
            pltpu.VMEM((width, 128), BF16),
            pltpu.VMEM((128, width), BF16),
            pltpu.SemaphoreType.DMA((8,)),
            pltpu.SemaphoreType.DMA((4,)),
            pltpu.VMEM((2, 2, 4, width), F32),
            pltpu.VMEM((2, 2, 4, width), F32),
            pltpu.VMEM((2, 4, 2, 2, XN, YN, 8, quarter), BF16),
            pltpu.VMEM((2, 2, 2, XN, YN, 8, quarter), BF16),
            pltpu.VMEM((2, 2, 2, XN, YN, 8, quarter), BF16),
            pltpu.VMEM((2, 2, 2, XN, YN, 8, quarter), BF16),
            pltpu.VMEM((2, 2, 2, YN, 8, quarter), BF16),
            pltpu.VMEM((2, 2, 3, 2, YN, 8, quarter), BF16),
            pltpu.VMEM((2, 2, 2, YN, 8, quarter), BF16),
            pltpu.VMEM((2, 2, 2, 8, quarter), BF16),
            pltpu.VMEM((2, 2, 3, 2, 8, quarter), BF16),
            pltpu.VMEM((2, 4, 4, half), BF16),
            pltpu.VMEM((2, 4, 4, half), BF16),
            pltpu.VMEM((2, 2, 4, half), F32),
            pltpu.VMEM((2, 2, 4, half), F32),
            pltpu.VMEM((2, 4, width), BF16),
            pltpu.VMEM((2, 4, width), BF16),
            pltpu.VMEM((2, 4, half), BF16),
            pltpu.VMEM((2, 4, half), BF16),
            pltpu.SemaphoreType.DMA((copies,)),
            pltpu.SemaphoreType.DMA((copies,)),
        ],
        compiler_params=pltpu.CompilerParams(
            collective_id=0, has_side_effects=True, vmem_limit_bytes=56 * 1024 * 1024
        ),
    )(
        x_down[:, 0], x_up[:, 0], g_down[0], g_up[0], loss_grad, w_in[0], w_out[0], gain, retention,
        layer_kind.reshape(1, -1),
    )
    down, up, grad_in, grad_out = pl.pallas_call(
        copy_out,
        out_shape=tuple(jax.ShapeDtypeStruct(a.shape, a.dtype) for a in results),
        in_specs=[anywhere] * 4,
        out_specs=(anywhere,) * 4,
        scratch_shapes=[pltpu.VMEM(a.shape, a.dtype) for a in results] + [pltpu.SemaphoreType.DMA((2, 4))],
    )(*results)
    return (down[None], up[None], grad_in[None], grad_out[None])


def solution(mesh):
    return jax.shard_map(
        body,
        mesh=mesh,
        in_specs=(
            P(None, "section", "tensor", None),
            P(None, "section", "tensor", None),
            P("section", "tensor", None),
            P("section", "tensor", None),
            P(None, "tensor", None),
            P("section", None, "tensor"),
            P("section", "tensor", None),
            P("section", None),
            P("section", "tensor"),
            P(),
        ),
        out_specs=(
            P("section", "tensor", None),
            P("section", "tensor", None),
            P("section", None, "tensor"),
            P("section", "tensor", None),
        ),
        check_vma=False,
    )
```

```python
import functools

import jax
import jax.numpy as jnp
from jax import lax
from jax.experimental import pallas as pl
from jax.experimental.pallas import tpu as pltpu
from jax.sharding import PartitionSpec as P

EPSILON = 1e-05
XN = 4
YN = 4
Y_DIRECT = False
X_DIRECT = False
SHARED_AT = 3
MESH = pl.DeviceIdType.MESH
F32 = jnp.float32
BF16 = jnp.bfloat16
HIGHEST = lax.Precision.HIGHEST

AG_SEMS = 24
RS_SEMS = 32


def kernel(
    sections, x_down_h, x_up_h, g_down_h, g_up_h, loss_h, w_in_h, w_out_h, gain_h, retention_h, kind_h,
    down_h, up_h, in_h, out_h,
    x_rows, g_rows, loss_rows, w_in, w_out, gain, retention, layer_kind, out_down, back_send, back_recv,
    out_in, out_out, load_sem, store_sem,
    xs, gs, gat, csend, crecv, part, xrelay, xfrom, yacc, yrelay, yfrom,
    pre_send, pre_recv, fin_send, fin_recv, hop_send, hop_recv, side_send, side_recv,
    send_sem, recv_sem,
):
    width = w_in.shape[0]
    half = width // 2
    quarter = width // 4
    loads = [
        pltpu.make_async_copy(src, dst, load_sem.at[i])
        for i, (src, dst) in enumerate((
            (x_down_h, x_rows.at[0]), (g_down_h, g_rows.at[0]), (gain_h, gain), (loss_h, loss_rows),
            (retention_h, retention), (kind_h, layer_kind), (w_in_h, w_in), (w_out_h, w_out),
        ))
    ]
    for copy in loads:
        copy.start()
    s = lax.axis_index("section")
    t = lax.axis_index("tensor")
    core = lax.rem(t, 2)
    y = lax.rem(t // 2, YN)
    x = t // (2 * YN)
    xr, xl, xo = lax.rem(x + 1, XN), lax.rem(x + 3, XN), lax.rem(x + 2, XN)
    yr, yl, yo = lax.rem(y + 1, YN), lax.rem(y + 3, YN), lax.rem(y + 2, YN)

    def tensor_id(xx, yy, cc):
        return (xx * YN + yy) * 2 + cc

    next_section = lax.rem(s + sections - 1, sections)
    prev_section = lax.rem(s + 1, sections)
    other = tensor_id(x, y, 1 - core)
    to_xr = (s, tensor_id(xr, y, core))
    to_xl = (s, tensor_id(xl, y, core))
    to_yr = (s, tensor_id(x, yr, core))
    to_yl = (s, tensor_id(x, yl, core))
    to_xo = (s, tensor_id(xo, y, core))
    to_yo = (s, tensor_id(x, yo, core))
    to_core = (s, other)
    to_mirror = (sections - 1 - s, t)
    to_next, to_next_side = (next_section, t), (next_section, other)
    to_prev, to_prev_side = (prev_section, t), (prev_section, other)

    barrier = pltpu.get_barrier_semaphore()
    peers = [
        to_xr, to_xl, to_yr, to_yl, to_core, to_mirror, to_next, to_prev, to_next_side, to_prev_side,
    ]
    if Y_DIRECT:
        peers.append(to_yo)
    if X_DIRECT:
        peers.append(to_xo)
    for peer in peers:
        pl.semaphore_signal(barrier, inc=1, device_id=peer, device_id_type=MESH)
    pl.semaphore_wait(barrier, len(peers))

    sent = []

    def send(src, dst, device):
        index = len(sent)
        copy = pltpu.make_async_remote_copy(
            src_ref=src, dst_ref=dst, send_sem=send_sem.at[index], recv_sem=recv_sem.at[index],
            device_id=device, device_id_type=MESH,
        )
        copy.start()
        sent.append(copy)
        return copy

    stores = []

    def store(src, dst):
        copy = pltpu.make_async_copy(src, dst, store_sem.at[len(stores)])
        copy.start()
        stores.append(copy)

    mx = send(x_up_h, x_rows.at[1], to_mirror)
    mg = send(g_up_h, g_rows.at[1], to_mirror)
    for copy in loads[:6]:
        copy.wait()

    gain_f = gain[...].astype(F32)
    rates = retention[...].astype(F32)
    lane_kind = lax.broadcasted_iota(jnp.int32, layer_kind.shape, 1)
    kind = jnp.sum(jnp.where(lane_kind == s, layer_kind[...], 0), axis=1, keepdims=True)
    is_attention = kind == 1
    first_core = core == 0

    def recip_of(rows):
        return lax.rsqrt(jnp.mean(rows * rows, axis=-1, keepdims=True) + EPSILON)

    def mine(rows):
        return jnp.where(first_core, rows[:, :half], rows[:, half:])

    def theirs(rows):
        return jnp.where(first_core, rows[:, half:], rows[:, :half])

    def put_unit(d, index, own, received):
        first = jnp.where(first_core, own, received)
        second = jnp.where(first_core, received, own)
        unit = jnp.concatenate([first, second], axis=0).astype(BF16)
        for q in range(2):
            gat[d, index, core, q, x, y] = unit[:, q * quarter:(q + 1) * quarter]

    def prepare(d):
        kept = []
        for tick in range(2):
            rows = x_rows[d, tick].astype(F32)
            xs[d, tick] = rows
            normed = (rows * recip_of(rows) * gain_f).astype(BF16).astype(F32)
            pre_send[d, 2 * tick] = theirs(normed).astype(BF16)
            kept.append(mine(normed))
        grads = g_rows[d].astype(F32)
        gs[d, 0] = grads
        pre_send[d, 1] = theirs(grads).astype(BF16)
        pre_send[d, 3] = theirs(loss_rows[d].astype(F32)).astype(BF16)
        copy = send(pre_send.at[d], pre_recv.at[d], to_core)
        copy.wait_recv()
        put_unit(d, 0, kept[0], pre_recv[d, 0].astype(F32))
        put_unit(d, 1, mine(grads), pre_recv[d, 1].astype(F32))
        put_unit(d, 2, kept[1], pre_recv[d, 2].astype(F32))

    def gather(directions, sets):
        def unit(xx, yy, q=None):
            if q is None:
                return gat.at[directions, sets, core, :, xx, yy]
            return gat.at[directions, sets, core, q, xx, yy]

        def spread_x(yy):
            ref = unit(x, yy)
            copies = [send(ref, ref, to_xr), send(ref, ref, to_xl)]
            if X_DIRECT:
                copies.append(send(ref, ref, to_xo))
            return copies

        def across(xx):
            ref = gat.at[directions, sets, core, :, xx]
            return send(ref, ref, to_core)

        own = unit(x, y)
        from_yl, from_yr = send(own, own, to_yr), send(own, own, to_yl)
        if Y_DIRECT:
            from_yo = [send(own, own, to_yo)]
        x_sends = [spread_x(y)]
        yield
        from_yl.wait_recv()
        if not Y_DIRECT:
            ref = unit(x, yl, 0)
            from_yo = [send(ref, ref, to_yr)]
        x_sends.append(spread_x(yl))
        from_yr.wait_recv()
        if not Y_DIRECT:
            ref = unit(x, yr, 1)
            from_yo.append(send(ref, ref, to_yl))
        x_sends.append(spread_x(yr))
        yield
        relays = []

        def relay_x(k, yy):
            x_sends[k][0].wait_recv()
            if not X_DIRECT:
                ref = unit(xl, yy, 0)
                relays.append(send(ref, ref, to_xr))
            x_sends[k][1].wait_recv()
            if not X_DIRECT:
                ref = unit(xr, yy, 1)
                relays.append(send(ref, ref, to_xl))

        if not Y_DIRECT:
            relay_x(0, y)
        for copy in from_yo:
            copy.wait_recv()
        x_sends.append(spread_x(yo))
        if Y_DIRECT:
            relay_x(0, y)
        crossing = [across(x)]
        yield
        relay_x(1, yl)
        relay_x(2, yr)
        yield
        relay_x(3, yo)
        crossing.append(across(xl))
        crossing.append(across(xr))
        yield
        for copy in relays:
            copy.wait_recv()
        if X_DIRECT:
            for copies in x_sends:
                copies[2].wait_recv()
        crossing.append(across(xo))
        yield
        for copy in crossing:
            copy.wait_recv()

    def gathered(d, index, i):
        return gat[d, index, i // 2, i % 2].reshape(128, quarter)

    def contract_last(left, right, **kw):
        return lax.dot_general(left, right, (((1,), (1,)), ((), ())), preferred_element_type=F32, **kw)

    def contract_first(left, right, **kw):
        return lax.dot_general(left, right, (((0,), (0,)), ((), ())), preferred_element_type=F32, **kw)

    def projected_of(d, index):
        total = 0.0
        for i in range(4):
            total = total + jnp.dot(
                gathered(d, index, i), w_in[i * quarter:(i + 1) * quarter, :], preferred_element_type=F32
            )
        return total

    def grad_mixed_of(d, index):
        total = 0.0
        for i in range(4):
            total = total + contract_last(gathered(d, index, i), w_out[:, i * quarter:(i + 1) * quarter])
        return total

    token = lax.broadcasted_iota(jnp.int32, (128, 128), 0)
    lane = lax.broadcasted_iota(jnp.int32, (128, 128), 1)
    causal = token >= lane
    low_lane = lane < 64

    def scan(values, backward):
        state = values
        power = rates
        step = 1
        while step < 128:
            if backward:
                moved = jnp.where(token < 128 - step, pltpu.roll(state, 128 - step, 0), 0.0)
            else:
                moved = jnp.where(token >= step, pltpu.roll(state, step, 0), 0.0)
            state = state + power * moved
            power = power * power
            step *= 2
        return state

    def mix_forward(v):
        state = scan((1.0 - rates) * v, False)
        gate = jax.nn.sigmoid(v)
        recurrent = state * (v * gate)
        turned = pltpu.roll(v, 64, 1)
        scores = contract_last(jnp.where(low_lane, v, 0.0), turned, precision=HIGHEST) * 0.125
        scores = jnp.where(causal, scores, -1e30)
        weights = jnp.exp(scores - jnp.max(scores, axis=-1, keepdims=True))
        weights = weights / jnp.sum(weights, axis=-1, keepdims=True)
        attended = jnp.dot(weights, v, precision=HIGHEST, preferred_element_type=F32)
        mixed = jnp.where(is_attention, attended, recurrent)
        return mixed.astype(BF16), (v, state, gate, weights)

    def mix_backward(saved, g):
        v, state, gate, weights = saved
        d_state = scan(g * (v * gate), True)
        recurrent = (1.0 - rates) * d_state + g * state * (gate * (1.0 + v * (1.0 - gate)))
        turned = pltpu.roll(v, 64, 1)
        d_weights = contract_last(g, v, precision=HIGHEST)
        d_scores = weights * (d_weights - jnp.sum(weights * d_weights, axis=-1, keepdims=True)) * 0.125
        d_query = jnp.dot(d_scores, turned, precision=HIGHEST, preferred_element_type=F32)
        d_key = contract_first(d_scores, v, precision=HIGHEST)
        attended = contract_first(weights, g, precision=HIGHEST) + jnp.where(
            low_lane, d_query, pltpu.roll(d_key, 64, 1)
        )
        return jnp.where(is_attention, attended, recurrent).astype(BF16)

    y_order = (yo, yr, yl, y)

    def add(*pieces):
        total = pieces[0].astype(F32)
        for piece in pieces[1:]:
            total = total + piece.astype(F32)
        return total

    def scatter(d, tick, grad_proj):
        def terms(which, q):
            at = pl.multiple_of(which * half + q * quarter, quarter)
            weights = w_in[pl.ds(at, quarter), :]
            return contract_last(grad_proj, weights).astype(BF16).reshape(XN, YN, 8, quarter)

        crossing = []
        for q in range(2):
            csend[d, tick, q] = terms(1 - core, q)
            crossing.append(send(csend.at[d, tick, q], crecv.at[d, tick, q], to_core))
        own = [terms(core, q) for q in range(2)]
        yield
        for q in range(2):
            crossing[q].wait_recv()
            part[d, tick, q] = add(own[q], crecv[d, tick, q]).astype(BF16)
        first, plain, joined = [], [], []
        p, xy, xf = part.at[d, tick], xrelay.at[d, tick], xfrom.at[d, tick]
        if X_DIRECT:
            for yy in y_order:
                plain.append([
                    send(p.at[:, xo, yy], xf.at[2, :, yy], to_xo),
                    send(p.at[:, xr, yy], xf.at[0, :, yy], to_xr),
                    send(p.at[:, xl, yy], xf.at[1, :, yy], to_xl),
                ])
                joined.append([])
            yield
        else:
            for yy in y_order:
                first.append((
                    send(p.at[0, xo, yy], xy.at[0, yy], to_xr),
                    send(p.at[1, xo, yy], xy.at[1, yy], to_xl),
                ))
            for yy in y_order:
                plain.append([
                    send(p.at[1, xr, yy], xf.at[0, 1, yy], to_xr),
                    send(p.at[0, xl, yy], xf.at[1, 0, yy], to_xl),
                ])
            yield
            for k, yy in enumerate(y_order):
                first[k][0].wait_recv()
                part[d, tick, 0, xr, yy] = add(part[d, tick, 0, xr, yy], xrelay[d, tick, 0, yy]).astype(BF16)
                right = send(p.at[0, xr, yy], xf.at[0, 0, yy], to_xr)
                first[k][1].wait_recv()
                part[d, tick, 1, xl, yy] = add(part[d, tick, 1, xl, yy], xrelay[d, tick, 1, yy]).astype(BF16)
                joined.append([right, send(p.at[1, xl, yy], xf.at[1, 1, yy], to_xl)])
                if k % 2 == 1:
                    yield

        def reduce_x(k):
            yy = y_order[k]
            for copy in plain[k] + joined[k]:
                copy.wait_recv()
            for q in range(2):
                pieces = [xfrom[d, tick, i, q, yy] for i in range(3 if X_DIRECT else 2)]
                yacc[d, tick, q, yy] = add(part[d, tick, q, x, yy], *pieces).astype(BF16)

        a, yrl, yf = yacc.at[d, tick], yrelay.at[d, tick], yfrom.at[d, tick]
        reduce_x(0)
        if Y_DIRECT:
            last = [send(a.at[:, yo], yf.at[2], to_yo)]
            reduce_x(1)
            last.append(send(a.at[:, yr], yf.at[0], to_yr))
            reduce_x(2)
            last.append(send(a.at[:, yl], yf.at[1], to_yl))
            reduce_x(3)
            yield
        else:
            first_r = send(a.at[0, yo], yrl.at[0], to_yr)
            first_l = send(a.at[1, yo], yrl.at[1], to_yl)
            reduce_x(1)
            last = [send(a.at[1, yr], yf.at[0, 1], to_yr)]
            reduce_x(2)
            last.append(send(a.at[0, yl], yf.at[1, 0], to_yl))
            reduce_x(3)
            yield
            first_r.wait_recv()
            yacc[d, tick, 0, yr] = add(yacc[d, tick, 0, yr], yrelay[d, tick, 0]).astype(BF16)
            last.append(send(a.at[0, yr], yf.at[0, 0], to_yr))
            first_l.wait_recv()
            yacc[d, tick, 1, yl] = add(yacc[d, tick, 1, yl], yrelay[d, tick, 1]).astype(BF16)
            last.append(send(a.at[1, yl], yf.at[1, 1], to_yl))
            yield
        for copy in last:
            copy.wait_recv()
        summed = jnp.concatenate([
            add(yacc[d, tick, q, y], *[yfrom[d, tick, i, q] for i in range(3 if Y_DIRECT else 2)])
            for q in range(2)
        ], axis=1)
        fin_send[d, tick] = jnp.where(first_core, summed[4:], summed[:4])
        swap = send(fin_send.at[d, tick], fin_recv.at[d, tick], to_core)
        kept = jnp.where(first_core, summed[:4], summed[4:])
        rows = xs[d, tick]
        recip = recip_of(rows)
        swap.wait_recv()
        received = fin_recv[d, tick]
        scaled = jnp.concatenate([
            jnp.where(first_core, kept, received), jnp.where(first_core, received, kept)
        ], axis=1) * gain_f
        along = jnp.mean(scaled * rows, axis=-1, keepdims=True)
        xs[d, tick] = gs[d, tick] + (recip * scaled - rows * (recip * recip * recip) * along)

    block = min(256, quarter)
    per_quarter = quarter // block

    def columns(d, index, i, at):
        return gat[d, index, i // 2, i % 2, :, :, :, pl.ds(at, block)].reshape(128, block)

    def both_ticks(d, index, i, at):
        return jnp.concatenate([columns(d, index, i, at), columns(d, index + 2, i, at)], axis=0)

    def weight_in(d, i, grad_both):
        def step(j, _):
            at = pl.multiple_of(j * block, block)
            rows = pl.ds(i * quarter + at, block)
            total = contract_first(both_ticks(d, 0, i, at), grad_both).astype(BF16)
            if d == 1:
                total = (out_in[rows, :].astype(F32) + total.astype(F32)).astype(BF16)
            out_in[rows, :] = total
            return 0

        lax.fori_loop(0, per_quarter, step, 0)

    def weight_out(d, i, mixed_turned):
        def step(j, _):
            at = pl.multiple_of(j * block, block)
            cols = pl.ds(i * quarter + at, block)
            total = jnp.dot(mixed_turned, both_ticks(d, 1, i, at), preferred_element_type=F32).astype(BF16)
            if d == 1:
                total = (out_out[:, cols].astype(F32) + total.astype(F32)).astype(BF16)
            out_out[:, cols] = total
            return 0

        lax.fori_loop(0, per_quarter, step, 0)

    def chain(d):
        one = pl.ds(d, 1)
        yield from gather(one, pl.ds(0, 2))
        if d == 0:
            loads[6].wait()
            loads[7].wait()
        mixed_1, saved = mix_forward(projected_of(d, 0))
        grad_proj_1 = mix_backward(saved, grad_mixed_of(d, 1))
        yield from scatter(d, 0, grad_proj_1)
        hop_send[d] = xs[d, 0].astype(BF16)
        side_send[d] = theirs(xs[d, 0]).astype(BF16)
        hop = send(hop_send.at[d], hop_recv.at[d], to_next)
        side = send(side_send.at[d], side_recv.at[d], to_next_side)
        yield "second"
        mixed_2, saved = mix_forward(projected_of(d, 2))
        mixed_turned = jnp.concatenate(
            [mixed_1.astype(F32), mixed_2.astype(F32)], axis=0
        ).T.astype(BF16)
        hop.wait_recv()
        side.wait_recv()
        at_top = s == sections - 1
        grads = jnp.where(at_top, loss_rows[d].astype(F32), hop_recv[d].astype(F32))
        gs[d, 1] = grads
        put_unit(
            d, 3, mine(grads),
            jnp.where(at_top, pre_recv[d, 3].astype(F32), side_recv[d].astype(F32)),
        )
        yield from gather(one, pl.ds(3, 1))
        grad_proj_2 = mix_backward(saved, grad_mixed_of(d, 3))
        steps = scatter(d, 1, grad_proj_2)
        grad_both = jnp.concatenate([grad_proj_1, grad_proj_2], axis=0)
        work = [functools.partial(weight_out, d, i, mixed_turned) for i in range(4)]
        work += [functools.partial(weight_in, d, i, grad_both) for i in range(4)]
        for _ in steps:
            yield
            if work:
                work.pop(0)()
        if d == 0:
            out_down[...] = xs[0, 1].astype(BF16)
            store(out_down, down_h)
        else:
            back_send[...] = xs[1, 1].astype(BF16)
            back = send(back_send, back_recv, to_mirror)
        while work:
            work.pop(0)()
        if d == 1:
            store(out_out, out_h)
            store(out_in, in_h)
            yield
            back.wait_recv()
            store(back_recv, up_h)

    prepare(0)
    down = chain(0)
    next(down)
    mx.wait_recv()
    mg.wait_recv()
    prepare(1)
    up = chain(1)
    shared = gather(pl.ds(0, 2), pl.ds(2, 1))
    turn = 0
    live = [down, up]
    while live:
        for steps in list(live):
            if next(steps, "end") == "second":
                for _ in shared:
                    pass
            if steps.gi_frame is None:
                live.remove(steps)
        turn += 1
        if turn >= SHARED_AT:
            next(shared, None)
    for copy in stores:
        copy.wait()
    for copy in sent:
        copy.wait_send()


def copy_out(*refs):
    sources, results, held, sem = refs[:4], refs[4:8], refs[8:12], refs[12]
    reads = [pltpu.make_async_copy(a, b, sem.at[0, i]) for i, (a, b) in enumerate(zip(sources, held))]
    writes = [pltpu.make_async_copy(a, b, sem.at[1, i]) for i, (a, b) in enumerate(zip(held, results))]
    for copy in reads:
        copy.start()
    for read, write in zip(reads, writes):
        read.wait()
        write.start()
    for copy in writes:
        copy.wait()


def body(x_down, x_up, g_down, g_up, loss_grad, w_in, w_out, gain, retention, layer_kind):
    sections = lax.axis_size("section")
    width = w_in.shape[1]
    half, quarter = width // 2, width // 4
    anywhere = pl.BlockSpec(memory_space=pl.ANY)
    copies = 5 * AG_SEMS + 4 * (RS_SEMS + 1) + 9
    results = pl.pallas_call(
        functools.partial(kernel, sections),
        out_shape=(
            jax.ShapeDtypeStruct((4, width), BF16),
            jax.ShapeDtypeStruct((4, width), BF16),
            jax.ShapeDtypeStruct((width, 128), BF16),
            jax.ShapeDtypeStruct((128, width), BF16),
        ),
        in_specs=[anywhere] * 10,
        out_specs=(anywhere,) * 4,
        scratch_shapes=[
            pltpu.VMEM((2, 2, 4, width), BF16),
            pltpu.VMEM((2, 4, width), BF16),
            pltpu.VMEM((2, 4, width), BF16),
            pltpu.VMEM((width, 128), BF16),
            pltpu.VMEM((128, width), BF16),
            pltpu.VMEM((1, width), BF16),
            pltpu.VMEM((1, 128), BF16),
            pltpu.VMEM((1, sections), jnp.int32),
            pltpu.VMEM((4, width), BF16),
            pltpu.VMEM((4, width), BF16),
            pltpu.VMEM((4, width), BF16),
            pltpu.VMEM((width, 128), BF16),
            pltpu.VMEM((128, width), BF16),
            pltpu.SemaphoreType.DMA((8,)),
            pltpu.SemaphoreType.DMA((4,)),
            pltpu.VMEM((2, 2, 4, width), F32),
            pltpu.VMEM((2, 2, 4, width), F32),
            pltpu.VMEM((2, 4, 2, 2, XN, YN, 8, quarter), BF16),
            pltpu.VMEM((2, 2, 2, XN, YN, 8, quarter), BF16),
            pltpu.VMEM((2, 2, 2, XN, YN, 8, quarter), BF16),
            pltpu.VMEM((2, 2, 2, XN, YN, 8, quarter), BF16),
            pltpu.VMEM((2, 2, 2, YN, 8, quarter), BF16),
            pltpu.VMEM((2, 2, 3, 2, YN, 8, quarter), BF16),
            pltpu.VMEM((2, 2, 2, YN, 8, quarter), BF16),
            pltpu.VMEM((2, 2, 2, 8, quarter), BF16),
            pltpu.VMEM((2, 2, 3, 2, 8, quarter), BF16),
            pltpu.VMEM((2, 4, 4, half), BF16),
            pltpu.VMEM((2, 4, 4, half), BF16),
            pltpu.VMEM((2, 2, 4, half), F32),
            pltpu.VMEM((2, 2, 4, half), F32),
            pltpu.VMEM((2, 4, width), BF16),
            pltpu.VMEM((2, 4, width), BF16),
            pltpu.VMEM((2, 4, half), BF16),
            pltpu.VMEM((2, 4, half), BF16),
            pltpu.SemaphoreType.DMA((copies,)),
            pltpu.SemaphoreType.DMA((copies,)),
        ],
        compiler_params=pltpu.CompilerParams(
            collective_id=0, has_side_effects=True, vmem_limit_bytes=56 * 1024 * 1024
        ),
    )(
        x_down[:, 0], x_up[:, 0], g_down[0], g_up[0], loss_grad, w_in[0], w_out[0], gain, retention,
        layer_kind.reshape(1, -1),
    )
    down, up, grad_in, grad_out = pl.pallas_call(
        copy_out,
        out_shape=tuple(jax.ShapeDtypeStruct(a.shape, a.dtype) for a in results),
        in_specs=[anywhere] * 4,
        out_specs=(anywhere,) * 4,
        scratch_shapes=[pltpu.VMEM(a.shape, a.dtype) for a in results] + [pltpu.SemaphoreType.DMA((2, 4))],
    )(*results)
    return (down[None], up[None], grad_in[None], grad_out[None])


def solution(mesh):
    return jax.shard_map(
        body,
        mesh=mesh,
        in_specs=(
            P(None, "section", "tensor", None),
            P(None, "section", "tensor", None),
            P("section", "tensor", None),
            P("section", "tensor", None),
            P(None, "tensor", None),
            P("section", None, "tensor"),
            P("section", "tensor", None),
            P("section", None),
            P("section", "tensor"),
            P(),
        ),
        out_specs=(
            P("section", "tensor", None),
            P("section", "tensor", None),
            P("section", None, "tensor"),
            P("section", "tensor", None),
        ),
        check_vma=False,
    )
```
